256 devices in a mesh: mem: 64 (over z, x, core), lev: 4 (over y).
Axes of the slice: x: 4, y: 4, z: 8, core: 2. Of those that a mesh axis runs over, the one named last changes fastest.
Arguments:
- hx_ens: bfloat16 [128, 524288], P('mem', 'lev'), may hold values from -6 to 6
- obs_value: float32 [524288], P('lev'), may hold values from -6 to 6
- obs_error: float32 [524288], P('lev'), may hold values from 0.7 to 1.4
- obs_list: int32 [1024, 1024], P(None, 'lev'), may hold values from 0 to 131071, as said below
- obs_count: int32 [1024, 4], P(None, 'lev'), may hold values from 192 to 256, as said below
- loc_class: int32 [1024, 1024], P(None, 'lev'), may hold values from 0 to 2
- state: bfloat16 [128, 1024, 4096], P('mem', None, 'lev'), may hold values from -6 to 6
Outputs:
- increment: bfloat16 [128, 1024, 4096], P('mem', None, 'lev')
The draws below stay inside these ranges and needn't reach their ends.
Inputs may be any that keep to these rules, and one draw needn't show every extreme that they name: `obs_list`: indices into the observations of the slot's level block, distinct within one patch's block of 256 slots; for patch p each index lies among the 384 indices that follow (p - 1) * 128 modulo 131072, that one included. `obs_count`: counts of the leading used slots; some patch and level block uses all 256 in every draw.
All inputs are finite; a program needn't handle non-finite values.
Results may differ from the reference program's by a relative error of at most 0.0076.
Values may be sent and summed in bfloat16 or wider, within the bound.
A program may use at most 128 MiB of HBM per device.

```python
import math
import jax
import jax.numpy as jnp
from jax import lax

K = 128
COLS = 512
ITERS = 6
CAP = 256
PATCHES = 1024
LEVELS = 8
OBS_PATCH = 128
NOBS_LEV = 131072
NOBS = 524288
N_LEV = 4


def draw_obs_list(key, part):
    key = jax.random.fold_in(key, 11)
    window = 3 * OBS_PATCH
    scores = jax.random.randint(key, (PATCHES, N_LEV, window), 0, 1 << 20)
    scores = scores * window + jnp.arange(window, dtype=jnp.int32)
    ranked = jnp.argsort(scores, axis=-1, stable=True)[:, :, :CAP].astype(jnp.int32)
    anchor = (jnp.arange(PATCHES, dtype=jnp.int32) - 1) * OBS_PATCH
    picked = (anchor[:, None, None] + ranked) % NOBS_LEV
    return picked.reshape(PATCHES, N_LEV * CAP).astype(jnp.int32)


def draw_obs_count(key, part):
    key = jax.random.fold_in(key, 12)
    head_key, tail_key = jax.random.split(key)
    counts = jax.random.randint(head_key, (PATCHES * N_LEV,), 3 * CAP // 4, CAP + 1)
    chosen = jax.random.randint(tail_key, (), 0, PATCHES * N_LEV)
    counts = jnp.where(jnp.arange(PATCHES * N_LEV, dtype=jnp.int32) == chosen, CAP, counts)
    return counts.reshape(PATCHES, N_LEV).astype(jnp.int32)


def plant(array, rng, smallest, top_value):
    longest = array.shape.index(max(array.shape))
    spots = []
    for shift in (0, 1):
        where = [jax.random.randint(jax.random.fold_in(rng, axis), (), 0, length) for axis, length in enumerate(array.shape)]
        where[longest] = (where[longest] + shift) % array.shape[longest]
        spots.append(tuple(where))
    return array.at[spots[0]].set(smallest).at[spots[1]].set(top_value)


def steps_of(key, extent, pieces, least, top_value):
    level = 1.0
    for position, parts in pieces:
        steps = jax.random.uniform(jax.random.fold_in(jax.random.fold_in(key, 6), position), (parts,), jnp.float32, least / len(pieces), top_value / len(pieces))
        level = level * jnp.repeat(jnp.exp(steps), extent[position] // parts).reshape((-1,) + (1,) * (len(extent) - 1 - position))
    return level


def bell_draw(rng, dims, scale, limit, pieces=(), kind=jnp.bfloat16):
    loudness = steps_of(rng, dims, pieces, -0.22, 0.18) if pieces else 1.0
    array = jax.random.normal(rng, dims, jnp.float32) * scale * loudness
    return jnp.minimum(jnp.maximum(array, -limit), limit).astype(kind)


def setup_inputs(seed: int = 0) -> dict:
    key_list = jax.random.split(jax.random.key(seed), 8)
    return {
        "hx_ens": bell_draw(key_list[0], (K, NOBS), 1.0, 6.0, ((0, 64), (1, 4))),
        "obs_value": bell_draw(key_list[1], (NOBS,), 1.0, 6.0, ((0, 4),), jnp.float32),
        "obs_error": jnp.clip(jnp.exp(math.log(1.4) - 0.6931472 * jax.random.uniform(key_list[2], (NOBS,), jnp.float32) ** steps_of(key_list[2], (NOBS,), ((0, 4),), -0.2, 0.2)), 0.7, 1.4),
        "obs_list": draw_obs_list(jax.random.fold_in(key_list[7], 71), 0),
        "obs_count": draw_obs_count(jax.random.fold_in(key_list[7], 71), 0),
        "loc_class": plant(jax.random.randint(key_list[5], (PATCHES, N_LEV * CAP), 0, 3), jax.random.fold_in(key_list[5], 1), 0, 2).astype(jnp.int32),
        "state": bell_draw(key_list[6], (K, PATCHES, LEVELS * COLS), 1.0, 6.0, ((0, 64), (2, 4))),
    }


highest = lax.Precision.HIGHEST

def inverse_root(matrix):
    size = matrix.shape[-1]
    identity = jnp.eye(size, dtype=jnp.float32)
    frob = jnp.sqrt(lax.optimization_barrier(jnp.sum(matrix * matrix, axis=(-2, -1), keepdims=True)))

    def sweep(index, carry):
        upper, lower = carry
        middle = 1.5 * identity - 0.5 * jnp.matmul(lower, upper, precision=highest)
        return (jnp.matmul(upper, middle, precision=highest), jnp.matmul(middle, lower, precision=highest))
    start = (matrix / frob, jnp.broadcast_to(identity, matrix.shape).astype(jnp.float32))
    upper, lower = lax.fori_loop(0, ITERS, sweep, start)
    return lower / jnp.sqrt(frob)

def mixing(gram, pull):
    size = gram.shape[-1]
    identity = jnp.eye(size, dtype=jnp.float32)
    system = gram + (size - 1.0) * identity
    root = inverse_root(system)
    covar = jnp.matmul(root, root, precision=highest)
    centre = lax.optimization_barrier(jnp.sum(covar * pull[..., None, :], axis=-1))
    weights = math.sqrt(size - 1.0) * root + centre[..., :, None] - identity
    return weights.astype(jnp.bfloat16)

def reference(hx_ens, obs_value, obs_error, obs_list, obs_count, loc_class, state):
    innov = (obs_value[None, :] - hx_ens.astype(jnp.float32)) / obs_error[None, :]
    slots = jnp.arange(N_LEV * CAP, dtype=jnp.int32)
    level_block = slots // CAP
    global_index = obs_list + (level_block * NOBS_LEV)[None, :]
    in_use = (slots % CAP)[None, :] < jnp.take(obs_count, level_block, axis=1)
    weight = jnp.exp(-0.5 * (loc_class.astype(jnp.float32) / 3.0) ** 2) * in_use.astype(jnp.float32)

    def analyse(patch):
        innov_rows = (jnp.take(innov, global_index[patch], axis=1) * weight[patch][None, :]).astype(jnp.bfloat16)
        values = innov_rows.astype(jnp.float32)
        average = lax.optimization_barrier(jnp.mean(values, axis=0))
        spread = values - average[None, :]
        gram = jnp.dot(spread, spread.T, precision=highest)
        pull = -jnp.dot(spread, average, precision=highest)
        mixer = mixing(gram, pull)
        column = lax.dynamic_index_in_dim(state, patch, 1, keepdims=False).astype(jnp.float32)
        anomaly = (column - lax.optimization_barrier(jnp.mean(column, axis=0))[None, :]).astype(jnp.bfloat16)
        return jnp.dot(mixer.T, anomaly, preferred_element_type=jnp.float32).astype(jnp.bfloat16)
    result = lax.map(analyse, jnp.arange(PATCHES, dtype=jnp.int32))
    return jnp.transpose(result, (1, 0, 2))
```

```python
import functools
import math

import jax
import jax.numpy as jnp
from jax import lax
from jax.experimental import pallas as pl
from jax.experimental.pallas import tpu as pltpu
from jax.sharding import PartitionSpec as P

ITERS = 6
MEMBERS = 128
GROUP = 64
LEVS = 4
PER = 16
QUART = PER // LEVS
HALF = 128
CAPACITY = 256
LEVEL_OBS = 131072
COLUMNS = 1024
CHUNKS = 4
WIDE = COLUMNS // CHUNKS
TILES = WIDE // 128
GRAM_ROWS = MEMBERS + 8

MESH = pl.DeviceIdType.MESH
HIGHEST = lax.Precision.HIGHEST
f32 = jnp.float32
bf16 = jnp.bfloat16


def dot_nt(a, b, precision=None):
    return lax.dot_general(
        a, b, (((1,), (1,)), ((), ())), precision=precision, preferred_element_type=f32
    )


def dot_nn(a, b, precision=None):
    return jnp.dot(a, b, precision=precision, preferred_element_type=f32)


def kernel(
    hx_ref, value_ref, error_ref, list_ref, count_ref, class_ref, state_ref,
    out_ref,
    hx_in, hx_rows, hx_win, obs_in, pieces, slot_in, count_in, weight,
    gram_out, gram_in, upper, lower, mixers,
    state_in, anomaly, product, result,
    hx_send, hx_recv, halo_send, halo_recv, local_sem,
    gram_send, gram_recv, mix_send, mix_recv,
    state_send, state_recv, out_send, out_recv,
):
    me = lax.axis_index("mem")
    lev = lax.axis_index("lev")
    depth, low = me // 8, me % 8
    before, after = (me + GROUP - 1) % GROUP, (me + 1) % GROUP

    barrier = pltpu.get_barrier_semaphore()

    @pl.loop(1, GROUP)
    def _(i):
        pl.semaphore_signal(barrier, inc=1, device_id=((me + i) % GROUP, lev), device_id_type=MESH)

    for i in range(1, LEVS):
        pl.semaphore_signal(barrier, inc=1, device_id=(me, (lev + i) % LEVS), device_id_type=MESH)

    local = []
    for k, source in enumerate((value_ref, error_ref)):
        for j, block in enumerate((before, me, after)):
            local.append(
                pltpu.make_async_copy(
                    source.at[pl.ds(block * PER, PER)], obs_in.at[k, pl.ds(j * PER, PER)],
                    local_sem.at[k * 3 + j],
                )
            )
    for k, source in enumerate((list_ref, class_ref)):
        local.append(
            pltpu.make_async_copy(source.at[pl.ds(me * PER, PER)], slot_in.at[k], local_sem.at[6 + k])
        )
    local.append(pltpu.make_async_copy(count_ref, count_in, local_sem.at[8]))
    for copy in local:
        copy.start()
    pltpu.make_async_copy(
        hx_ref.at[:, pl.ds(me * PER, PER)], hx_in.at[pl.ds(me * 2, 2)], hx_recv
    ).start()
    for q in range(CHUNKS):
        cols = pl.ds(q * WIDE, WIDE)
        pltpu.make_async_copy(
            state_ref.at[:, pl.ds(me * PER, PER), cols], state_in.at[q, pl.ds(me * 2, 2)], state_recv.at[q]
        ).start()

    pl.semaphore_wait(barrier, GROUP - 1 + LEVS - 1)

    def to_all(send):
        @pl.loop(0, 8)
        def _(j):
            for dz in (4, 1, 7, 2, 6, 3, 5, 0):
                target = ((depth + dz) % 8) * 8 + (low + j) % 8
                if dz == 0:

                    @pl.when(j > 0)
                    def _():
                        send(target)
                else:
                    send(target)

    def send_hx(target):
        pltpu.make_async_remote_copy(
            src_ref=hx_ref.at[:, pl.ds(target * PER, PER)],
            dst_ref=hx_in.at[pl.ds(me * 2, 2)],
            send_sem=hx_send, recv_sem=hx_recv, device_id=(target, lev), device_id_type=MESH,
        ).start()

    to_all(send_hx)

    for q in range(CHUNKS):

        def send_state(target, q=q):
            pltpu.make_async_remote_copy(
                src_ref=state_ref.at[:, pl.ds(target * PER, PER), pl.ds(q * WIDE, WIDE)],
                dst_ref=state_in.at[q, pl.ds(me * 2, 2)],
                send_sem=state_send, recv_sem=state_recv.at[q],
                device_id=(target, lev), device_id_type=MESH,
            ).start()

        to_all(send_state)

    for copy in local:
        copy.wait()
    lanes = lax.broadcasted_iota(jnp.int32, (8, 128), 1)
    rows8 = lax.broadcasted_iota(jnp.int32, (8, 128), 0)
    mine = jnp.sum(jnp.where(rows8 == me // 8, count_in[...], 0), axis=0, keepdims=True)
    spots = lax.broadcasted_iota(jnp.int32, (PER, 128), 1) - (me % 8) * PER
    patch_rows = lax.broadcasted_iota(jnp.int32, (PER, 128), 0)
    counts = jnp.sum(jnp.where(spots == patch_rows, mine, 0), axis=1, keepdims=True)
    slots = lax.broadcasted_iota(jnp.int32, (PER, CAPACITY), 1)
    scaled = slot_in[1].astype(f32) / 3.0
    weight[...] = jnp.where(slots < counts, jnp.exp(-0.5 * (scaled * scaled)), 0.0)
    del lanes
    for k in range(2):
        rest = obs_in[k]
        for j in range(3):
            piece = rest.astype(bf16).astype(f32)
            pieces[k * 3 + j] = piece
            rest = rest - piece

    pltpu.make_async_copy(hx_in, hx_in, hx_recv).wait()
    hx_rows[...] = hx_in[...].astype(f32).reshape(MEMBERS * PER, 128)

    def take_block(b):
        hx_win[b + 1] = hx_rows[pl.ds(b, MEMBERS, stride=PER), :].astype(bf16)

    for b in range(PER):
        take_block(b)
    halo = [
        pltpu.make_async_remote_copy(
            src_ref=hx_win.at[1], dst_ref=hx_win.at[PER + 1],
            send_sem=halo_send.at[0], recv_sem=halo_recv.at[0],
            device_id=(before, lev), device_id_type=MESH,
        ),
        pltpu.make_async_remote_copy(
            src_ref=hx_win.at[PER], dst_ref=hx_win.at[0],
            send_sem=halo_send.at[1], recv_sem=halo_recv.at[1],
            device_id=(after, lev), device_id_type=MESH,
        ),
    ]
    for copy in halo:
        copy.start()

    def patch_gram(p):
        anchor = (me * PER + p - 1) * HALF
        offset = (slot_in[0, pl.ds(p, 1), :] - anchor) & (LEVEL_OBS - 1)
        places = lax.broadcasted_iota(jnp.int32, (HALF, CAPACITY), 0)
        chosen = jnp.zeros((MEMBERS, CAPACITY), f32)
        observed = jnp.zeros((8, CAPACITY), f32)
        for j in range(3):
            table = jnp.where(places + j * HALF == offset, 1.0, 0.0).astype(bf16)
            chosen += dot_nn(hx_win[p + j], table)
            parts = [pieces[k, pl.ds(PER - 1 + p + j, 1), :] for k in range(6)]
            stack = jnp.concatenate(parts + [jnp.zeros((2, HALF), f32)], axis=0)
            observed += dot_nn(stack.astype(bf16), table)
        value = observed[0:1] + observed[1:2] + observed[2:3]
        error = observed[3:4] + observed[4:5] + observed[5:6]
        innov = ((value - chosen) / error * weight[pl.ds(p, 1), :]).astype(bf16).astype(f32)
        average = jnp.mean(innov, axis=0, keepdims=True)
        spread = innov - average
        both = jnp.concatenate([spread, jnp.broadcast_to(average, (8, CAPACITY))], axis=0)
        gram_out[p] = dot_nt(both, spread, HIGHEST)

    @pl.loop(1, PER - 1)
    def _(p):
        patch_gram(p)

    for copy in halo:
        copy.wait()

    @pl.loop(0, 2)
    def _(i):
        patch_gram(i * (PER - 1))

    gram_copies = []
    for i in range(1, LEVS):
        target = (lev + i) % LEVS
        gram_copies.append(
            pltpu.make_async_remote_copy(
                src_ref=gram_out.at[pl.ds(target * QUART, QUART)],
                dst_ref=gram_in.at[i - 1],
                send_sem=gram_send.at[i - 1], recv_sem=gram_recv.at[i - 1],
                device_id=(me, target), device_id_type=MESH,
            )
        )
    for copy in gram_copies:
        copy.start()
    for copy in gram_copies:
        copy.wait()

    diagonal = lax.broadcasted_iota(jnp.int32, (MEMBERS, MEMBERS), 0) == lax.broadcasted_iota(
        jnp.int32, (MEMBERS, MEMBERS), 1
    )
    identity = jnp.where(diagonal, 1.0, 0.0).astype(f32)
    frobs, pulls = [], []
    for k in range(QUART):
        total = gram_out[lev * QUART + k] + gram_in[0, k] + gram_in[1, k] + gram_in[2, k]
        system = total[:MEMBERS] + (MEMBERS - 1.0) * identity
        squares = jnp.sum(jnp.sum(system * system, axis=0, keepdims=True), axis=1, keepdims=True)
        frob = jnp.sqrt(squares)
        frobs.append(frob)
        pulls.append(-total[MEMBERS : MEMBERS + 1])
        upper[k] = system / frob
        lower[k] = identity

    @pl.loop(0, ITERS)
    def _(step):
        middles = [
            1.5 * identity - 0.5 * dot_nn(lower[k], upper[k], HIGHEST) for k in range(QUART)
        ]
        uppers = [dot_nn(upper[k], middles[k], HIGHEST) for k in range(QUART)]
        lowers = [dot_nn(middles[k], lower[k], HIGHEST) for k in range(QUART)]
        for k in range(QUART):
            upper[k] = uppers[k]
            lower[k] = lowers[k]

    for k in range(QUART):
        root = lower[k] / jnp.sqrt(frobs[k])
        covar = dot_nn(root, root, HIGHEST)
        centre = jnp.sum(covar * pulls[k], axis=1, keepdims=True)
        mixer = math.sqrt(MEMBERS - 1.0) * root + centre - identity
        mixers[lev * QUART + k] = mixer.T.astype(bf16)

    mix_copies = []
    for i in range(1, LEVS):
        target = (lev + i) % LEVS
        mix_copies.append(
            pltpu.make_async_remote_copy(
                src_ref=mixers.at[pl.ds(lev * QUART, QUART)],
                dst_ref=mixers.at[pl.ds(lev * QUART, QUART)],
                send_sem=mix_send.at[i - 1], recv_sem=mix_recv.at[i - 1],
                device_id=(me, target), device_id_type=MESH,
            )
        )
    for copy in mix_copies:
        copy.start()
    for copy in mix_copies:
        copy.wait()

    for q in range(CHUNKS):
        cols = pl.ds(q * WIDE, WIDE)
        pltpu.make_async_copy(state_in.at[q], state_in.at[q], state_recv.at[q]).wait()
        for t in range(TILES):
            tile = slice(t * 128, (t + 1) * 128)

            def add(i, total):
                block = state_in[q, pl.ds(i * 8, 8), :, tile].astype(f32)
                return total + jnp.sum(block, axis=0)

            total = lax.fori_loop(0, MEMBERS // 8, add, jnp.zeros((PER, 128), f32))
            mean = total / MEMBERS

            @pl.loop(0, MEMBERS // 8)
            def _(i):
                block = state_in[q, pl.ds(i * 8, 8), :, tile].astype(f32) - mean[None]
                anomaly[t, pl.ds(i * 8 * PER, 8 * PER), :] = block.reshape(8 * PER, 128)

        for p in range(PER):
            right = jnp.concatenate(
                [anomaly[t, pl.ds(p, MEMBERS, stride=PER), :] for t in range(TILES)], axis=1
            ).astype(bf16)
            left = dot_nn(mixers[p], right)
            for t in range(TILES):
                product[t, pl.ds(p, MEMBERS, stride=PER), :] = left[:, t * 128 : (t + 1) * 128]

        for t in range(TILES):
            tile = slice(t * 128, (t + 1) * 128)

            @pl.loop(0, MEMBERS // 8)
            def _(i):
                block = product[t, pl.ds(i * 8 * PER, 8 * PER), :]
                result[q, pl.ds(i * 8, 8), :, tile] = block.reshape(8, PER, 128).astype(bf16)

        pltpu.make_async_copy(
            result.at[q, pl.ds(me * 2, 2)], out_ref.at[:, pl.ds(me * PER, PER), cols], out_recv
        ).start()

        def send_result(target, q=q, cols=cols):
            pltpu.make_async_remote_copy(
                src_ref=result.at[q, pl.ds(target * 2, 2)],
                dst_ref=out_ref.at[:, pl.ds(me * PER, PER), cols],
                send_sem=out_send, recv_sem=out_recv,
                device_id=(target, lev), device_id_type=MESH,
            ).start()

        to_all(send_result)

    others = GROUP - 1
    pltpu.make_async_copy(
        hx_in.at[pl.ds(0, 2 * others)], hx_in.at[pl.ds(0, 2 * others)], hx_send
    ).wait()
    sent = state_ref.at[:, pl.ds(0, PER * others)]
    pltpu.make_async_copy(sent, sent, state_send).wait()
    pltpu.make_async_copy(sent, sent, out_send).wait()
    pltpu.make_async_copy(out_ref, out_ref, out_recv).wait()


def body(hx_ens, obs_value, obs_error, obs_list, obs_count, loc_class, state):
    blocks = LEVEL_OBS // HALF
    dma = pltpu.SemaphoreType.DMA
    any_space = pl.BlockSpec(memory_space=pl.ANY)
    return pl.pallas_call(
        kernel,
        out_shape=jax.ShapeDtypeStruct(state.shape, bf16),
        in_specs=[any_space] * 7,
        out_specs=any_space,
        scratch_shapes=[
            pltpu.VMEM((MEMBERS, PER, 128), bf16),
            pltpu.VMEM((MEMBERS * PER, 128), f32),
            pltpu.VMEM((PER + 2, MEMBERS, 128), bf16),
            pltpu.VMEM((2, 3 * PER, 128), f32),
            pltpu.VMEM((6, 3 * PER, 128), f32),
            pltpu.VMEM((2, PER, CAPACITY), jnp.int32),
            pltpu.VMEM((8, 128), jnp.int32),
            pltpu.VMEM((PER, CAPACITY), f32),
            pltpu.VMEM((PER, GRAM_ROWS, MEMBERS), f32),
            pltpu.VMEM((LEVS - 1, QUART, GRAM_ROWS, MEMBERS), f32),
            pltpu.VMEM((QUART, MEMBERS, MEMBERS), f32),
            pltpu.VMEM((QUART, MEMBERS, MEMBERS), f32),
            pltpu.VMEM((PER, MEMBERS, MEMBERS), bf16),
            pltpu.VMEM((CHUNKS, MEMBERS, PER, WIDE), bf16),
            pltpu.VMEM((TILES, MEMBERS * PER, 128), f32),
            pltpu.VMEM((TILES, MEMBERS * PER, 128), f32),
            pltpu.VMEM((CHUNKS, MEMBERS, PER, WIDE), bf16),
            dma, dma, dma((2,)), dma((2,)), dma((9,)),
            dma((3,)), dma((3,)), dma((3,)), dma((3,)),
            dma, dma((CHUNKS,)), dma, dma,
        ],
        compiler_params=pltpu.CompilerParams(
            collective_id=0, has_side_effects=True, vmem_limit_bytes=48 << 20
        ),
        cost_estimate=pl.CostEstimate(flops=2_000_000_000, bytes_accessed=20_000_000, transcendentals=0),
    )(
        hx_ens.reshape(2, blocks, HALF),
        obs_value.reshape(blocks, HALF),
        obs_error.reshape(blocks, HALF),
        obs_list,
        obs_count.reshape(8, 128),
        loc_class,
        state,
    )


def solution(mesh):
    return jax.shard_map(
        body,
        mesh=mesh,
        in_specs=(
            P("mem", "lev"),
            P("lev"),
            P("lev"),
            P(None, "lev"),
            P(None, "lev"),
            P(None, "lev"),
            P("mem", None, "lev"),
        ),
        out_specs=P("mem", None, "lev"),
        check_vma=False,
    )
```

```python
import functools
import math

import jax
import jax.numpy as jnp
from jax import lax
from jax.experimental import pallas as pl
from jax.experimental.pallas import tpu as pltpu
from jax.sharding import PartitionSpec as P

ITERS = 6
MEMBERS = 128
GROUP = 64
LEVS = 4
PER = 16
QUART = PER // LEVS
HALF = 128
CAPACITY = 256
LEVEL_OBS = 131072
COLUMNS = 1024
CHUNKS = 4
WIDE = COLUMNS // CHUNKS
TILES = WIDE // 128
GRAM_ROWS = MEMBERS + 8

MESH = pl.DeviceIdType.MESH
HIGHEST = lax.Precision.HIGHEST
f32 = jnp.float32
bf16 = jnp.bfloat16


def dot_nt(a, b, precision=None):
    return lax.dot_general(
        a, b, (((1,), (1,)), ((), ())), precision=precision, preferred_element_type=f32
    )


def dot_nn(a, b, precision=None):
    return jnp.dot(a, b, precision=precision, preferred_element_type=f32)


def kernel(
    hx_ref, value_ref, error_ref, list_ref, count_ref, class_ref, state_ref,
    out_ref,
    hx_in, hx_rows, hx_win, obs_in, pieces, slot_in, count_in, weight,
    gram_out, gram_in, upper, lower, mixers,
    state_in, anomaly, product, result,
    hx_send, hx_recv, halo_send, halo_recv, local_sem,
    gram_send, gram_recv, mix_send, mix_recv,
    state_send, state_recv, out_send, out_recv,
):
    me = lax.axis_index("mem")
    lev = lax.axis_index("lev")
    depth, low = me // 8, me % 8
    before, after = (me + GROUP - 1) % GROUP, (me + 1) % GROUP

    barrier = pltpu.get_barrier_semaphore()

    @pl.loop(1, GROUP)
    def _(i):
        pl.semaphore_signal(barrier, inc=1, device_id=((me + i) % GROUP, lev), device_id_type=MESH)

    for i in range(1, LEVS):
        pl.semaphore_signal(barrier, inc=1, device_id=(me, (lev + i) % LEVS), device_id_type=MESH)

    local = []
    for k, source in enumerate((value_ref, error_ref)):
        for j, block in enumerate((before, me, after)):
            local.append(
                pltpu.make_async_copy(
                    source.at[pl.ds(block * PER, PER)], obs_in.at[k, pl.ds(j * PER, PER)],
                    local_sem.at[k * 3 + j],
                )
            )
    for k, source in enumerate((list_ref, class_ref)):
        local.append(
            pltpu.make_async_copy(source.at[pl.ds(me * PER, PER)], slot_in.at[k], local_sem.at[6 + k])
        )
    local.append(pltpu.make_async_copy(count_ref, count_in, local_sem.at[8]))
    for copy in local:
        copy.start()
    pltpu.make_async_copy(
        hx_ref.at[:, pl.ds(me * PER, PER)], hx_in.at[pl.ds(me * 2, 2)], hx_recv
    ).start()
    for q in range(CHUNKS):
        cols = pl.ds(q * WIDE, WIDE)
        pltpu.make_async_copy(
            state_ref.at[:, pl.ds(me * PER, PER), cols], state_in.at[q, pl.ds(me * 2, 2)], state_recv.at[q]
        ).start()

    pl.semaphore_wait(barrier, GROUP - 1 + LEVS - 1)

    def to_all(send):
        @pl.loop(0, 8)
        def _(j):
            for dz in (4, 1, 7, 2, 6, 3, 5, 0):
                target = ((depth + dz) % 8) * 8 + (low + j) % 8
                if dz == 0:

                    @pl.when(j > 0)
                    def _():
                        send(target)
                else:
                    send(target)

    def send_hx(target):
        pltpu.make_async_remote_copy(
            src_ref=hx_ref.at[:, pl.ds(target * PER, PER)],
            dst_ref=hx_in.at[pl.ds(me * 2, 2)],
            send_sem=hx_send, recv_sem=hx_recv, device_id=(target, lev), device_id_type=MESH,
        ).start()

    to_all(send_hx)

    for q in range(CHUNKS):

        def send_state(target, q=q):
            pltpu.make_async_remote_copy(
                src_ref=state_ref.at[:, pl.ds(target * PER, PER), pl.ds(q * WIDE, WIDE)],
                dst_ref=state_in.at[q, pl.ds(me * 2, 2)],
                send_sem=state_send, recv_sem=state_recv.at[q],
                device_id=(target, lev), device_id_type=MESH,
            ).start()

        to_all(send_state)

    for copy in local:
        copy.wait()
    lanes = lax.broadcasted_iota(jnp.int32, (8, 128), 1)
    rows8 = lax.broadcasted_iota(jnp.int32, (8, 128), 0)
    mine = jnp.sum(jnp.where(rows8 == me // 8, count_in[...], 0), axis=0, keepdims=True)
    spots = lax.broadcasted_iota(jnp.int32, (PER, 128), 1) - (me % 8) * PER
    patch_rows = lax.broadcasted_iota(jnp.int32, (PER, 128), 0)
    counts = jnp.sum(jnp.where(spots == patch_rows, mine, 0), axis=1, keepdims=True)
    slots = lax.broadcasted_iota(jnp.int32, (PER, CAPACITY), 1)
    scaled = slot_in[1].astype(f32) / 3.0
    weight[...] = jnp.where(slots < counts, jnp.exp(-0.5 * (scaled * scaled)), 0.0)
    del lanes
    for k in range(2):
        rest = obs_in[k]
        for j in range(3):
            piece = rest.astype(bf16).astype(f32)
            pieces[k * 3 + j] = piece
            rest = rest - piece

    pltpu.make_async_copy(hx_in, hx_in, hx_recv).wait()
    hx_rows[...] = hx_in[...].astype(f32).reshape(MEMBERS * PER, 128)

    def take_block(b):
        hx_win[b + 1] = hx_rows[pl.ds(b, MEMBERS, stride=PER), :].astype(bf16)

    for b in range(PER):
        take_block(b)
    halo = [
        pltpu.make_async_remote_copy(
            src_ref=hx_win.at[1], dst_ref=hx_win.at[PER + 1],
            send_sem=halo_send.at[0], recv_sem=halo_recv.at[0],
            device_id=(before, lev), device_id_type=MESH,
        ),
        pltpu.make_async_remote_copy(
            src_ref=hx_win.at[PER], dst_ref=hx_win.at[0],
            send_sem=halo_send.at[1], recv_sem=halo_recv.at[1],
            device_id=(after, lev), device_id_type=MESH,
        ),
    ]
    for copy in halo:
        copy.start()

    def patch_gram(p):
        anchor = (me * PER + p - 1) * HALF
        offset = (slot_in[0, pl.ds(p, 1), :] - anchor) & (LEVEL_OBS - 1)
        places = lax.broadcasted_iota(jnp.int32, (HALF, CAPACITY), 0)
        chosen = jnp.zeros((MEMBERS, CAPACITY), f32)
        observed = jnp.zeros((8, CAPACITY), f32)
        for j in range(3):
            table = jnp.where(places + j * HALF == offset, 1.0, 0.0).astype(bf16)
            chosen += dot_nn(hx_win[p + j], table)
            parts = [pieces[k, pl.ds(PER - 1 + p + j, 1), :] for k in range(6)]
            stack = jnp.concatenate(parts + [jnp.zeros((2, HALF), f32)], axis=0)
            observed += dot_nn(stack.astype(bf16), table)
        value = observed[0:1] + observed[1:2] + observed[2:3]
        error = observed[3:4] + observed[4:5] + observed[5:6]
        innov = ((value - chosen) / error * weight[pl.ds(p, 1), :]).astype(bf16).astype(f32)
        average = jnp.mean(innov, axis=0, keepdims=True)
        spread = innov - average
        both = jnp.concatenate([spread, jnp.broadcast_to(average, (8, CAPACITY))], axis=0)
        gram_out[p] = dot_nt(both, spread, HIGHEST)

    @pl.loop(1, PER - 1)
    def _(p):
        patch_gram(p)

    for copy in halo:
        copy.wait()

    @pl.loop(0, 2)
    def _(i):
        patch_gram(i * (PER - 1))

    gram_copies = []
    for i in range(1, LEVS):
        target = (lev + i) % LEVS
        gram_copies.append(
            pltpu.make_async_remote_copy(
                src_ref=gram_out.at[pl.ds(target * QUART, QUART)],
                dst_ref=gram_in.at[i - 1],
                send_sem=gram_send.at[i - 1], recv_sem=gram_recv.at[i - 1],
                device_id=(me, target), device_id_type=MESH,
            )
        )
    for copy in gram_copies:
        copy.start()
    for copy in gram_copies:
        copy.wait()

    diagonal = lax.broadcasted_iota(jnp.int32, (MEMBERS, MEMBERS), 0) == lax.broadcasted_iota(
        jnp.int32, (MEMBERS, MEMBERS), 1
    )
    identity = jnp.where(diagonal, 1.0, 0.0).astype(f32)
    frobs, pulls = [], []
    for k in range(QUART):
        total = gram_out[lev * QUART + k] + gram_in[0, k] + gram_in[1, k] + gram_in[2, k]
        system = total[:MEMBERS] + (MEMBERS - 1.0) * identity
        squares = jnp.sum(jnp.sum(system * system, axis=0, keepdims=True), axis=1, keepdims=True)
        frob = jnp.sqrt(squares)
        frobs.append(frob)
        pulls.append(-total[MEMBERS : MEMBERS + 1])
        upper[k] = system / frob
        lower[k] = identity

    @pl.loop(0, ITERS)
    def _(step):
        middles = [
            1.5 * identity - 0.5 * dot_nn(lower[k], upper[k], HIGHEST) for k in range(QUART)
        ]
        uppers = [dot_nn(upper[k], middles[k], HIGHEST) for k in range(QUART)]
        lowers = [dot_nn(middles[k], lower[k], HIGHEST) for k in range(QUART)]
        for k in range(QUART):
            upper[k] = uppers[k]
            lower[k] = lowers[k]

    for k in range(QUART):
        root = lower[k] / jnp.sqrt(frobs[k])
        covar = dot_nn(root, root, HIGHEST)
        centre = jnp.sum(covar * pulls[k], axis=1, keepdims=True)
        mixer = math.sqrt(MEMBERS - 1.0) * root + centre - identity
        mixers[lev * QUART + k] = mixer.T.astype(bf16)

    mix_copies = []
    for i in range(1, LEVS):
        target = (lev + i) % LEVS
        mix_copies.append(
            pltpu.make_async_remote_copy(
                src_ref=mixers.at[pl.ds(lev * QUART, QUART)],
                dst_ref=mixers.at[pl.ds(lev * QUART, QUART)],
                send_sem=mix_send.at[i - 1], recv_sem=mix_recv.at[i - 1],
                device_id=(me, target), device_id_type=MESH,
            )
        )
    for copy in mix_copies:
        copy.start()
    for copy in mix_copies:
        copy.wait()

    for q in range(CHUNKS):
        cols = pl.ds(q * WIDE, WIDE)
        pltpu.make_async_copy(state_in.at[q], state_in.at[q], state_recv.at[q]).wait()
        for t in range(TILES):
            tile = slice(t * 128, (t + 1) * 128)

            def add(i, total):
                block = state_in[q, pl.ds(i * 8, 8), :, tile].astype(f32)
                return total + jnp.sum(block, axis=0)

            total = lax.fori_loop(0, MEMBERS // 8, add, jnp.zeros((PER, 128), f32))
            mean = total / MEMBERS

            @pl.loop(0, MEMBERS // 8)
            def _(i):
                block = state_in[q, pl.ds(i * 8, 8), :, tile].astype(f32) - mean[None]
                anomaly[t, pl.ds(i * 8 * PER, 8 * PER), :] = block.reshape(8 * PER, 128)

        for p in range(PER):
            right = jnp.concatenate(
                [anomaly[t, pl.ds(p, MEMBERS, stride=PER), :] for t in range(TILES)], axis=1
            ).astype(bf16)
            left = dot_nn(mixers[p], right)
            for t in range(TILES):
                product[t, pl.ds(p, MEMBERS, stride=PER), :] = left[:, t * 128 : (t + 1) * 128]

        for t in range(TILES):
            tile = slice(t * 128, (t + 1) * 128)

            @pl.loop(0, MEMBERS // 8)
            def _(i):
                block = product[t, pl.ds(i * 8 * PER, 8 * PER), :]
                result[q, pl.ds(i * 8, 8), :, tile] = block.reshape(8, PER, 128).astype(bf16)

        pltpu.make_async_copy(
            result.at[q, pl.ds(me * 2, 2)], out_ref.at[:, pl.ds(me * PER, PER), cols], out_recv
        ).start()

        def send_result(target, q=q, cols=cols):
            pltpu.make_async_remote_copy(
                src_ref=result.at[q, pl.ds(target * 2, 2)],
                dst_ref=out_ref.at[:, pl.ds(me * PER, PER), cols],
                send_sem=out_send, recv_sem=out_recv,
                device_id=(target, lev), device_id_type=MESH,
            ).start()

        to_all(send_result)

    others = GROUP - 1
    pltpu.make_async_copy(
        hx_in.at[pl.ds(0, 2 * others)], hx_in.at[pl.ds(0, 2 * others)], hx_send
    ).wait()
    sent = state_ref.at[:, pl.ds(0, PER * others)]
    pltpu.make_async_copy(sent, sent, state_send).wait()
    pltpu.make_async_copy(sent, sent, out_send).wait()
    pltpu.make_async_copy(out_ref, out_ref, out_recv).wait()


def body(hx_ens, obs_value, obs_error, obs_list, obs_count, loc_class, state):
    blocks = LEVEL_OBS // HALF
    dma = pltpu.SemaphoreType.DMA
    any_space = pl.BlockSpec(memory_space=pltpu.HBM)
    return pl.pallas_call(
        kernel,
        out_shape=pltpu.VMEM(state.shape, bf16),
        in_specs=[any_space] * 7,
        out_specs=pl.BlockSpec(memory_space=pltpu.VMEM),
        scratch_shapes=[
            pltpu.VMEM((MEMBERS, PER, 128), bf16),
            pltpu.VMEM((MEMBERS * PER, 128), f32),
            pltpu.VMEM((PER + 2, MEMBERS, 128), bf16),
            pltpu.VMEM((2, 3 * PER, 128), f32),
            pltpu.VMEM((6, 3 * PER, 128), f32),
            pltpu.VMEM((2, PER, CAPACITY), jnp.int32),
            pltpu.VMEM((8, 128), jnp.int32),
            pltpu.VMEM((PER, CAPACITY), f32),
            pltpu.VMEM((PER, GRAM_ROWS, MEMBERS), f32),
            pltpu.VMEM((LEVS - 1, QUART, GRAM_ROWS, MEMBERS), f32),
            pltpu.VMEM((QUART, MEMBERS, MEMBERS), f32),
            pltpu.VMEM((QUART, MEMBERS, MEMBERS), f32),
            pltpu.VMEM((PER, MEMBERS, MEMBERS), bf16),
            pltpu.VMEM((CHUNKS, MEMBERS, PER, WIDE), bf16),
            pltpu.VMEM((TILES, MEMBERS * PER, 128), f32),
            pltpu.VMEM((TILES, MEMBERS * PER, 128), f32),
            pltpu.VMEM((CHUNKS, MEMBERS, PER, WIDE), bf16),
            dma, dma, dma((2,)), dma((2,)), dma((9,)),
            dma((3,)), dma((3,)), dma((3,)), dma((3,)),
            dma, dma((CHUNKS,)), dma, dma,
        ],
        compiler_params=pltpu.CompilerParams(
            collective_id=0, has_side_effects=True, vmem_limit_bytes=40 << 20
        ),
        cost_estimate=pl.CostEstimate(flops=2_000_000_000, bytes_accessed=20_000_000, transcendentals=0),
    )(
        *(
            pltpu.with_memory_space_constraint(operand, pltpu.HBM)
            for operand in (
                hx_ens.reshape(2, blocks, HALF),
                obs_value.reshape(blocks, HALF),
                obs_error.reshape(blocks, HALF),
                obs_list,
                obs_count.reshape(8, 128),
                loc_class,
                state,
            )
        )
    )


def solution(mesh):
    return jax.shard_map(
        body,
        mesh=mesh,
        in_specs=(
            P("mem", "lev"),
            P("lev"),
            P("lev"),
            P(None, "lev"),
            P(None, "lev"),
            P(None, "lev"),
            P("mem", None, "lev"),
        ),
        out_specs=P("mem", None, "lev"),
        check_vma=False,
    )
```

```python
import functools
import math

import jax
import jax.numpy as jnp
from jax import lax
from jax.experimental import pallas as pl
from jax.experimental.pallas import tpu as pltpu
from jax.sharding import PartitionSpec as P

ITERS = 6
MEMBERS = 128
GROUP = 64
LEVS = 4
PER = 16
QUART = PER // LEVS
HALF = 128
CAPACITY = 256
LEVEL_OBS = 131072
COLUMNS = 1024
CHUNKS = 4
WIDE = COLUMNS // CHUNKS
TILES = WIDE // 128
GRAM_ROWS = MEMBERS + 8

MESH = pl.DeviceIdType.MESH
HIGHEST = lax.Precision.HIGHEST
f32 = jnp.float32
bf16 = jnp.bfloat16


def dot_nt(a, b, precision=None):
    return lax.dot_general(
        a, b, (((1,), (1,)), ((), ())), precision=precision, preferred_element_type=f32
    )


def dot_nn(a, b, precision=None):
    return jnp.dot(a, b, precision=precision, preferred_element_type=f32)


def kernel(
    hx_ref, value_ref, error_ref, list_ref, count_ref, class_ref, state_ref,
    out_ref,
    hx_in, hx_win, obs_in, pieces, slot_in, count_in, weight,
    gram_out, gram_in, upper, lower, mixers,
    state_in, anomaly, product, result,
    hx_send, hx_recv, halo_send, halo_recv, local_sem,
    gram_send, gram_recv, mix_send, mix_recv,
    state_send, state_recv, out_send, out_recv,
):
    me = lax.axis_index("mem")
    lev = lax.axis_index("lev")
    depth, low = me // 8, me % 8
    before, after = (me + GROUP - 1) % GROUP, (me + 1) % GROUP

    barrier = pltpu.get_barrier_semaphore()

    @pl.loop(1, GROUP)
    def _(i):
        pl.semaphore_signal(barrier, inc=1, device_id=((me + i) % GROUP, lev), device_id_type=MESH)

    for i in range(1, LEVS):
        pl.semaphore_signal(barrier, inc=1, device_id=(me, (lev + i) % LEVS), device_id_type=MESH)

    local = []
    for k, source in enumerate((value_ref, error_ref)):
        for j, block in enumerate((before, me, after)):
            local.append(
                pltpu.make_async_copy(
                    source.at[pl.ds(block * PER, PER)], obs_in.at[k, pl.ds(j * PER, PER)],
                    local_sem.at[k * 3 + j],
                )
            )
    for k, source in enumerate((list_ref, class_ref)):
        local.append(
            pltpu.make_async_copy(source.at[pl.ds(me * PER, PER)], slot_in.at[k], local_sem.at[6 + k])
        )
    local.append(pltpu.make_async_copy(count_ref, count_in, local_sem.at[8]))
    for copy in local:
        copy.start()
    pltpu.make_async_copy(
        hx_ref.at[pl.ds(me * PER, PER)], hx_in.at[me], hx_recv
    ).start()
    for q in range(CHUNKS):
        cols = pl.ds(q * WIDE, WIDE)
        pltpu.make_async_copy(
            state_ref.at[:, pl.ds(me * PER, PER), cols], state_in.at[q, pl.ds(me * 2, 2)], state_recv.at[q]
        ).start()

    pl.semaphore_wait(barrier, GROUP - 1 + LEVS - 1)

    def to_all(send):
        @pl.loop(0, 8)
        def _(j):
            for dz in (4, 1, 7, 2, 6, 3, 5, 0):
                target = ((depth + dz) % 8) * 8 + (low + j) % 8
                if dz == 0:

                    @pl.when(j > 0)
                    def _():
                        send(target)
                else:
                    send(target)

    def send_hx(target):
        pltpu.make_async_remote_copy(
            src_ref=hx_ref.at[pl.ds(target * PER, PER)],
            dst_ref=hx_in.at[me],
            send_sem=hx_send, recv_sem=hx_recv, device_id=(target, lev), device_id_type=MESH,
        ).start()

    to_all(send_hx)

    for q in range(CHUNKS):

        def send_state(target, q=q):
            pltpu.make_async_remote_copy(
                src_ref=state_ref.at[:, pl.ds(target * PER, PER), pl.ds(q * WIDE, WIDE)],
                dst_ref=state_in.at[q, pl.ds(me * 2, 2)],
                send_sem=state_send, recv_sem=state_recv.at[q],
                device_id=(target, lev), device_id_type=MESH,
            ).start()

        to_all(send_state)

    for copy in local:
        copy.wait()
    lanes = lax.broadcasted_iota(jnp.int32, (8, 128), 1)
    rows8 = lax.broadcasted_iota(jnp.int32, (8, 128), 0)
    mine = jnp.sum(jnp.where(rows8 == me // 8, count_in[...], 0), axis=0, keepdims=True)
    spots = lax.broadcasted_iota(jnp.int32, (PER, 128), 1) - (me % 8) * PER
    patch_rows = lax.broadcasted_iota(jnp.int32, (PER, 128), 0)
    counts = jnp.sum(jnp.where(spots == patch_rows, mine, 0), axis=1, keepdims=True)
    slots = lax.broadcasted_iota(jnp.int32, (PER, CAPACITY), 1)
    scaled = slot_in[1].astype(f32) / 3.0
    weight[...] = jnp.where(slots < counts, jnp.exp(-0.5 * (scaled * scaled)), 0.0)
    del lanes
    for k in range(2):
        rest = obs_in[k]
        for j in range(3):
            piece = rest.astype(bf16).astype(f32)
            pieces[k * 3 + j] = piece
            rest = rest - piece

    pltpu.make_async_copy(hx_in, hx_in, hx_recv).wait()

    def take_block(b):
        hx_win[b + 1] = hx_in[:, b].astype(f32).reshape(MEMBERS, 128).astype(bf16)

    for b in range(PER):
        take_block(b)
    halo = [
        pltpu.make_async_remote_copy(
            src_ref=hx_win.at[1], dst_ref=hx_win.at[PER + 1],
            send_sem=halo_send.at[0], recv_sem=halo_recv.at[0],
            device_id=(before, lev), device_id_type=MESH,
        ),
        pltpu.make_async_remote_copy(
            src_ref=hx_win.at[PER], dst_ref=hx_win.at[0],
            send_sem=halo_send.at[1], recv_sem=halo_recv.at[1],
            device_id=(after, lev), device_id_type=MESH,
        ),
    ]
    for copy in halo:
        copy.start()

    def patch_gram(p):
        anchor = (me * PER + p - 1) * HALF
        offset = (slot_in[0, pl.ds(p, 1), :] - anchor) & (LEVEL_OBS - 1)
        places = lax.broadcasted_iota(jnp.int32, (HALF, CAPACITY), 0)
        chosen = jnp.zeros((MEMBERS, CAPACITY), f32)
        observed = jnp.zeros((8, CAPACITY), f32)
        for j in range(3):
            table = jnp.where(places + j * HALF == offset, 1.0, 0.0).astype(bf16)
            chosen += dot_nn(hx_win[p + j], table)
            parts = [pieces[k, pl.ds(PER - 1 + p + j, 1), :] for k in range(6)]
            stack = jnp.concatenate(parts + [jnp.zeros((2, HALF), f32)], axis=0)
            observed += dot_nn(stack.astype(bf16), table)
        value = observed[0:1] + observed[1:2] + observed[2:3]
        error = observed[3:4] + observed[4:5] + observed[5:6]
        innov = ((value - chosen) / error * weight[pl.ds(p, 1), :]).astype(bf16).astype(f32)
        average = jnp.mean(innov, axis=0, keepdims=True)
        spread = innov - average
        both = jnp.concatenate([spread, jnp.broadcast_to(average, (8, CAPACITY))], axis=0)
        gram_out[p] = dot_nt(both, spread, HIGHEST)

    @pl.loop(1, PER - 1)
    def _(p):
        patch_gram(p)

    for copy in halo:
        copy.wait()

    @pl.loop(0, 2)
    def _(i):
        patch_gram(i * (PER - 1))

    gram_copies = []
    for i in range(1, LEVS):
        target = (lev + i) % LEVS
        gram_copies.append(
            pltpu.make_async_remote_copy(
                src_ref=gram_out.at[pl.ds(target * QUART, QUART)],
                dst_ref=gram_in.at[i - 1],
                send_sem=gram_send.at[i - 1], recv_sem=gram_recv.at[i - 1],
                device_id=(me, target), device_id_type=MESH,
            )
        )
    for copy in gram_copies:
        copy.start()
    for copy in gram_copies:
        copy.wait()

    diagonal = lax.broadcasted_iota(jnp.int32, (MEMBERS, MEMBERS), 0) == lax.broadcasted_iota(
        jnp.int32, (MEMBERS, MEMBERS), 1
    )
    identity = jnp.where(diagonal, 1.0, 0.0).astype(f32)
    frobs, pulls = [], []
    for k in range(QUART):
        total = gram_out[lev * QUART + k] + gram_in[0, k] + gram_in[1, k] + gram_in[2, k]
        system = total[:MEMBERS] + (MEMBERS - 1.0) * identity
        squares = jnp.sum(jnp.sum(system * system, axis=0, keepdims=True), axis=1, keepdims=True)
        frob = jnp.sqrt(squares)
        frobs.append(frob)
        pulls.append(-total[MEMBERS : MEMBERS + 1])
        upper[k] = system / frob
        lower[k] = identity

    @pl.loop(0, ITERS)
    def _(step):
        middles = [
            1.5 * identity - 0.5 * dot_nn(lower[k], upper[k], HIGHEST) for k in range(QUART)
        ]
        uppers = [dot_nn(upper[k], middles[k], HIGHEST) for k in range(QUART)]
        lowers = [dot_nn(middles[k], lower[k], HIGHEST) for k in range(QUART)]
        for k in range(QUART):
            upper[k] = uppers[k]
            lower[k] = lowers[k]

    for k in range(QUART):
        root = lower[k] / jnp.sqrt(frobs[k])
        covar = dot_nn(root, root, HIGHEST)
        centre = jnp.sum(covar * pulls[k], axis=1, keepdims=True)
        mixer = math.sqrt(MEMBERS - 1.0) * root + centre - identity
        mixers[lev * QUART + k] = mixer.T.astype(bf16)

    mix_copies = []
    for i in range(1, LEVS):
        target = (lev + i) % LEVS
        mix_copies.append(
            pltpu.make_async_remote_copy(
                src_ref=mixers.at[pl.ds(lev * QUART, QUART)],
                dst_ref=mixers.at[pl.ds(lev * QUART, QUART)],
                send_sem=mix_send.at[i - 1], recv_sem=mix_recv.at[i - 1],
                device_id=(me, target), device_id_type=MESH,
            )
        )
    for copy in mix_copies:
        copy.start()
    for copy in mix_copies:
        copy.wait()

    for q in range(CHUNKS):
        cols = pl.ds(q * WIDE, WIDE)
        pltpu.make_async_copy(state_in.at[q], state_in.at[q], state_recv.at[q]).wait()
        for t in range(TILES):
            tile = slice(t * 128, (t + 1) * 128)

            def add(i, total):
                block = state_in[q, pl.ds(i * 8, 8), :, tile].astype(f32)
                return total + jnp.sum(block, axis=0)

            total = lax.fori_loop(0, MEMBERS // 8, add, jnp.zeros((PER, 128), f32))
            mean = total / MEMBERS

            @pl.loop(0, MEMBERS // 8)
            def _(i):
                block = state_in[q, pl.ds(i * 8, 8), :, tile].astype(f32) - mean[None]
                anomaly[t, pl.ds(i * 8 * PER, 8 * PER), :] = block.reshape(8 * PER, 128)

        for p in range(PER):
            right = jnp.concatenate(
                [anomaly[t, pl.ds(p, MEMBERS, stride=PER), :] for t in range(TILES)], axis=1
            ).astype(bf16)
            left = dot_nn(mixers[p], right)
            for t in range(TILES):
                product[t, pl.ds(p, MEMBERS, stride=PER), :] = left[:, t * 128 : (t + 1) * 128]

        for t in range(TILES):
            tile = slice(t * 128, (t + 1) * 128)

            @pl.loop(0, MEMBERS // 8)
            def _(i):
                block = product[t, pl.ds(i * 8 * PER, 8 * PER), :]
                result[q, pl.ds(i * 8, 8), :, tile] = block.reshape(8, PER, 128).astype(bf16)

        pltpu.make_async_copy(
            result.at[q, pl.ds(me * 2, 2)], out_ref.at[:, pl.ds(me * PER, PER), cols], out_recv
        ).start()

        def send_result(target, q=q, cols=cols):
            pltpu.make_async_remote_copy(
                src_ref=result.at[q, pl.ds(target * 2, 2)],
                dst_ref=out_ref.at[:, pl.ds(me * PER, PER), cols],
                send_sem=out_send, recv_sem=out_recv,
                device_id=(target, lev), device_id_type=MESH,
            ).start()

        to_all(send_result)

    others = GROUP - 1
    pltpu.make_async_copy(
        hx_in.at[pl.ds(0, others)], hx_in.at[pl.ds(0, others)], hx_send
    ).wait()
    sent = state_ref.at[:, pl.ds(0, PER * others)]
    pltpu.make_async_copy(sent, sent, state_send).wait()
    pltpu.make_async_copy(sent, sent, out_send).wait()
    pltpu.make_async_copy(out_ref, out_ref, out_recv).wait()


def body(hx_ens, obs_value, obs_error, obs_list, obs_count, loc_class, state):
    blocks = LEVEL_OBS // HALF
    dma = pltpu.SemaphoreType.DMA
    any_space = pl.BlockSpec(memory_space=pltpu.HBM)
    return pl.pallas_call(
        kernel,
        out_shape=pltpu.VMEM(state.shape, bf16),
        in_specs=[any_space] * 7,
        out_specs=pl.BlockSpec(memory_space=pltpu.VMEM),
        scratch_shapes=[
            pltpu.VMEM((GROUP, PER, 2, 128), bf16),
            pltpu.VMEM((PER + 2, MEMBERS, 128), bf16),
            pltpu.VMEM((2, 3 * PER, 128), f32),
            pltpu.VMEM((6, 3 * PER, 128), f32),
            pltpu.VMEM((2, PER, CAPACITY), jnp.int32),
            pltpu.VMEM((8, 128), jnp.int32),
            pltpu.VMEM((PER, CAPACITY), f32),
            pltpu.VMEM((PER, GRAM_ROWS, MEMBERS), f32),
            pltpu.VMEM((LEVS - 1, QUART, GRAM_ROWS, MEMBERS), f32),
            pltpu.VMEM((QUART, MEMBERS, MEMBERS), f32),
            pltpu.VMEM((QUART, MEMBERS, MEMBERS), f32),
            pltpu.VMEM((PER, MEMBERS, MEMBERS), bf16),
            pltpu.VMEM((CHUNKS, MEMBERS, PER, WIDE), bf16),
            pltpu.VMEM((TILES, MEMBERS * PER, 128), f32),
            pltpu.VMEM((TILES, MEMBERS * PER, 128), f32),
            pltpu.VMEM((CHUNKS, MEMBERS, PER, WIDE), bf16),
            dma, dma, dma((2,)), dma((2,)), dma((9,)),
            dma((3,)), dma((3,)), dma((3,)), dma((3,)),
            dma, dma((CHUNKS,)), dma, dma,
        ],
        compiler_params=pltpu.CompilerParams(
            collective_id=0, has_side_effects=True, vmem_limit_bytes=40 << 20
        ),
        cost_estimate=pl.CostEstimate(flops=2_000_000_000, bytes_accessed=20_000_000, transcendentals=0),
    )(
        *(
            pltpu.with_memory_space_constraint(operand, pltpu.HBM)
            for operand in (
                hx_ens.reshape(2, blocks, HALF).transpose(1, 0, 2),
                obs_value.reshape(blocks, HALF),
                obs_error.reshape(blocks, HALF),
                obs_list,
                obs_count.reshape(8, 128),
                loc_class,
                state,
            )
        )
    )


def solution(mesh):
    return jax.shard_map(
        body,
        mesh=mesh,
        in_specs=(
            P("mem", "lev"),
            P("lev"),
            P("lev"),
            P(None, "lev"),
            P(None, "lev"),
            P(None, "lev"),
            P("mem", None, "lev"),
        ),
        out_specs=P("mem", None, "lev"),
        check_vma=False,
    )
```

```python
import functools
import math

import jax
import jax.numpy as jnp
from jax import lax
from jax.experimental import pallas as pl
from jax.experimental.pallas import tpu as pltpu
from jax.sharding import PartitionSpec as P

ITERS = 6
MEMBERS = 128
PLANES = 8
SITES = 8
SHARE = 2
LEVS = 4
PER = 16
AREA = PER * SITES
QUART = PER // LEVS
HALF = 128
CAPACITY = 256
LEVEL_OBS = 131072
COLUMNS = 1024
CHUNKS = 8
WIDE = COLUMNS // CHUNKS
TILES = WIDE // 128
GRAM_ROWS = MEMBERS + 8
Z_ORDER = (1, 7, 2, 6, 3, 5, 4)
X_ORDER = (1, 7, 2, 6, 3, 5, 4)
EARLY = CHUNKS // 4

MESH = pl.DeviceIdType.MESH
HIGHEST = lax.Precision.HIGHEST
f32 = jnp.float32
bf16 = jnp.bfloat16


def dot_nt(a, b, precision=None):
    return lax.dot_general(
        a, b, (((1,), (1,)), ((), ())), precision=precision, preferred_element_type=f32
    )


def dot_nn(a, b, precision=None):
    return jnp.dot(a, b, precision=precision, preferred_element_type=f32)


def kernel(
    hx_ref, value_ref, error_ref, list_ref, count_ref, class_ref, state_ref,
    out_ref,
    hx_plane, hx_in, hx_win, obs_in, pieces, slot_in, count_in, weight,
    gram_out, gram_in, upper, lower, mixers,
    state_plane, state_in, anomaly, product, result, result_plane,
    hx_z_send, hx_z_recv, hx_x_send, hx_x_recv, local_sem,
    gram_send, gram_recv, mix_send, mix_recv,
    state_z_send, state_z_recv, state_x_send, state_x_recv,
    out_x_send, out_x_recv, out_z_send, out_z_recv,
):
    me = lax.axis_index("mem")
    lev = lax.axis_index("lev")
    plane, site = lax.div(me, SITES), lax.rem(me, SITES)
    before, after = lax.rem(me + 63, 64), lax.rem(me + 1, 64)

    def along_z(step):
        there = lax.rem(plane + step, PLANES)
        return there, (there * SITES + site, lev)

    def in_plane(step):
        there = lax.rem(site + step, SITES)
        return there, (plane * SITES + there, lev)

    def greet(device):
        pl.semaphore_signal(barrier, inc=1, device_id=device, device_id_type=MESH)

    barrier = pltpu.get_barrier_semaphore()
    for step in range(1, PLANES):
        greet(along_z(step)[1])
    for step in range(1, SITES):
        greet(in_plane(step)[1])
    for step in range(1, LEVS):
        greet((me, lax.rem(lev + step, LEVS)))

    local = []
    for k, source in enumerate((value_ref, error_ref)):
        for j, block in enumerate((before, me, after)):
            local.append(
                pltpu.make_async_copy(
                    source.at[pl.ds(block * PER, PER)], obs_in.at[k, pl.ds(j * PER, PER)],
                    local_sem.at[k * 3 + j],
                )
            )
    for k, source in enumerate((list_ref, class_ref)):
        local.append(
            pltpu.make_async_copy(source.at[pl.ds(me * PER, PER)], slot_in.at[k], local_sem.at[6 + k])
        )
    local.append(pltpu.make_async_copy(count_ref, count_in, local_sem.at[8]))
    for copy in local:
        copy.start()
    for q in range(CHUNKS):
        pltpu.make_async_copy(
            state_ref.at[:, pl.ds(plane * AREA, AREA), pl.ds(q * WIDE, WIDE)],
            state_plane.at[q, pl.ds(plane * SHARE, SHARE)],
            state_z_recv.at[q],
        ).start()

    def hx_pieces(there):
        blocks = LEVEL_OBS // HALF
        first = there * AREA
        return (
            (hx_ref.at[pl.ds(first, AREA)], hx_plane.at[plane, pl.ds(1, AREA)]),
            (hx_ref.at[pl.ds(lax.rem(first + blocks - 1, blocks), 1)], hx_plane.at[plane, pl.ds(0, 1)]),
            (hx_ref.at[pl.ds(lax.rem(first + AREA, blocks), 1)], hx_plane.at[plane, pl.ds(AREA + 1, 1)]),
        )

    for source, target in hx_pieces(plane):
        pltpu.make_async_copy(source, target, hx_z_recv).start()

    pl.semaphore_wait(barrier, PLANES - 1 + SITES - 1 + LEVS - 1)

    def remote(source, target, send_sem, recv_sem, device):
        pltpu.make_async_remote_copy(
            src_ref=source, dst_ref=target, send_sem=send_sem, recv_sem=recv_sem,
            device_id=device, device_id_type=MESH,
        ).start()

    for step in Z_ORDER:
        there, device = along_z(step)
        for source, target in hx_pieces(there):
            remote(source, target, hx_z_send, hx_z_recv, device)

    def send_state(q):
        for step in Z_ORDER:
            there, device = along_z(step)
            remote(
                state_ref.at[:, pl.ds(there * AREA, AREA), pl.ds(q * WIDE, WIDE)],
                state_plane.at[q, pl.ds(plane * SHARE, SHARE)],
                state_z_send, state_z_recv.at[q], device,
            )

    def pass_state(q):
        pltpu.make_async_copy(state_plane.at[q], state_plane.at[q], state_z_recv.at[q]).wait()
        for step in X_ORDER:
            there, device = in_plane(step)
            remote(
                state_plane.at[q, :, pl.ds(there * PER, PER)],
                state_in.at[q, pl.ds(site * 16, 16)],
                state_x_send, state_x_recv.at[q], device,
            )
        pltpu.make_async_copy(
            state_plane.at[q, :, pl.ds(site * PER, PER)],
            state_in.at[q, pl.ds(site * 16, 16)],
            state_x_recv.at[q],
        ).start()

    for q in range(CHUNKS):
        send_state(q)

    for copy in local:
        copy.wait()
    lanes = lax.broadcasted_iota(jnp.int32, (8, 128), 1)
    rows8 = lax.broadcasted_iota(jnp.int32, (8, 128), 0)
    mine = jnp.sum(jnp.where(rows8 == lax.div(me, 8), count_in[...], 0), axis=0, keepdims=True)
    spots = lax.broadcasted_iota(jnp.int32, (PER, 128), 1) - lax.rem(me, 8) * PER
    patch_rows = lax.broadcasted_iota(jnp.int32, (PER, 128), 0)
    counts = jnp.sum(jnp.where(spots == patch_rows, mine, 0), axis=1, keepdims=True)
    slots = lax.broadcasted_iota(jnp.int32, (PER, CAPACITY), 1)
    scaled = slot_in[1].astype(f32) / 3.0
    weight[...] = jnp.where(slots < counts, jnp.exp(-0.5 * (scaled * scaled)), 0.0)
    del lanes
    for k in range(2):
        rest = obs_in[k]
        for j in range(3):
            piece = rest.astype(bf16).astype(f32)
            pieces[k * 3 + j] = piece
            rest = rest - piece

    pltpu.make_async_copy(hx_plane, hx_plane, hx_z_recv).wait()
    for step in X_ORDER:
        there, device = in_plane(step)
        remote(
            hx_plane.at[:, pl.ds(there * PER, PER + 2)], hx_in.at[site], hx_x_send, hx_x_recv, device
        )
    pltpu.make_async_copy(
        hx_plane.at[:, pl.ds(site * PER, PER + 2)], hx_in.at[site], hx_x_recv
    ).start()
    pltpu.make_async_copy(hx_in, hx_in, hx_x_recv).wait()
    for b in range(PER + 2):
        hx_win[b] = hx_in[:, :, b].astype(f32).reshape(MEMBERS, 128).astype(bf16)

    def patch_gram(p):
        anchor = (me * PER + p - 1) * HALF
        offset = (slot_in[0, pl.ds(p, 1), :] - anchor) & (LEVEL_OBS - 1)
        places = lax.broadcasted_iota(jnp.int32, (HALF, CAPACITY), 0)
        chosen = jnp.zeros((MEMBERS, CAPACITY), f32)
        observed = jnp.zeros((8, CAPACITY), f32)
        for j in range(3):
            table = jnp.where(places + j * HALF == offset, 1.0, 0.0).astype(bf16)
            chosen += dot_nn(hx_win[p + j], table)
            parts = [pieces[k, pl.ds(PER - 1 + p + j, 1), :] for k in range(6)]
            stack = jnp.concatenate(parts + [jnp.zeros((2, HALF), f32)], axis=0)
            observed += dot_nn(stack.astype(bf16), table)
        value = observed[0:1] + observed[1:2] + observed[2:3]
        error = observed[3:4] + observed[4:5] + observed[5:6]
        innov = ((value - chosen) / error * weight[pl.ds(p, 1), :]).astype(bf16).astype(f32)
        average = jnp.mean(innov, axis=0, keepdims=True)
        spread = innov - average
        both = jnp.concatenate([spread, jnp.broadcast_to(average, (8, CAPACITY))], axis=0)
        gram_out[p] = dot_nt(both, spread, HIGHEST)

    @pl.loop(0, PER)
    def _(p):
        patch_gram(p)

    gram_copies = []
    for i in range(1, LEVS):
        target = lax.rem(lev + i, LEVS)
        gram_copies.append(
            pltpu.make_async_remote_copy(
                src_ref=gram_out.at[pl.ds(target * QUART, QUART)],
                dst_ref=gram_in.at[i - 1],
                send_sem=gram_send.at[i - 1], recv_sem=gram_recv.at[i - 1],
                device_id=(me, target), device_id_type=MESH,
            )
        )
    for copy in gram_copies:
        copy.start()
    for q in range(EARLY):
        pass_state(q)
    for copy in gram_copies:
        copy.wait()

    diagonal = lax.broadcasted_iota(jnp.int32, (MEMBERS, MEMBERS), 0) == lax.broadcasted_iota(
        jnp.int32, (MEMBERS, MEMBERS), 1
    )
    identity = jnp.where(diagonal, 1.0, 0.0).astype(f32)
    frobs, pulls = [], []
    for k in range(QUART):
        total = gram_out[lev * QUART + k] + gram_in[0, k] + gram_in[1, k] + gram_in[2, k]
        system = total[:MEMBERS] + (MEMBERS - 1.0) * identity
        squares = jnp.sum(jnp.sum(system * system, axis=0, keepdims=True), axis=1, keepdims=True)
        frob = jnp.sqrt(squares)
        frobs.append(frob)
        pulls.append(-total[MEMBERS : MEMBERS + 1])
        upper[k] = system / frob
        lower[k] = identity

    @pl.loop(0, ITERS)
    def _(step):
        middles = [
            1.5 * identity - 0.5 * dot_nn(lower[k], upper[k], HIGHEST) for k in range(QUART)
        ]
        uppers = [dot_nn(upper[k], middles[k], HIGHEST) for k in range(QUART)]
        lowers = [dot_nn(middles[k], lower[k], HIGHEST) for k in range(QUART)]
        for k in range(QUART):
            upper[k] = uppers[k]
            lower[k] = lowers[k]

    for k in range(QUART):
        root = lower[k] / jnp.sqrt(frobs[k])
        covar = dot_nn(root, root, HIGHEST)
        centre = jnp.sum(covar * pulls[k], axis=1, keepdims=True)
        mixer = math.sqrt(MEMBERS - 1.0) * root + centre - identity
        mixers[lev * QUART + k] = mixer.T.astype(bf16)

    mix_copies = []
    for i in range(1, LEVS):
        target = lax.rem(lev + i, LEVS)
        mix_copies.append(
            pltpu.make_async_remote_copy(
                src_ref=mixers.at[pl.ds(lev * QUART, QUART)],
                dst_ref=mixers.at[pl.ds(lev * QUART, QUART)],
                send_sem=mix_send.at[i - 1], recv_sem=mix_recv.at[i - 1],
                device_id=(me, target), device_id_type=MESH,
            )
        )
    for copy in mix_copies:
        copy.start()
    for q in range(EARLY, 2 * EARLY):
        pass_state(q)
    for copy in mix_copies:
        copy.wait()

    def apply(q):
        pltpu.make_async_copy(state_in.at[q], state_in.at[q], state_x_recv.at[q]).wait()
        for t in range(TILES):
            tile = slice(t * 128, (t + 1) * 128)

            def add(i, total):
                block = state_in[q, pl.ds(i * 8, 8), :, tile].astype(f32)
                return total + jnp.sum(block, axis=0)

            total = lax.fori_loop(0, MEMBERS // 8, add, jnp.zeros((PER, 128), f32))
            mean = total / MEMBERS

            @pl.loop(0, MEMBERS // 8)
            def _(i):
                block = state_in[q, pl.ds(i * 8, 8), :, tile].astype(f32) - mean[None]
                anomaly[t, pl.ds(i * 8 * PER, 8 * PER), :] = block.reshape(8 * PER, 128)

        for p in range(PER):
            right = jnp.concatenate(
                [anomaly[t, pl.ds(p, MEMBERS, stride=PER), :] for t in range(TILES)], axis=1
            ).astype(bf16)
            left = dot_nn(mixers[p], right)
            for t in range(TILES):
                product[t, pl.ds(p, MEMBERS, stride=PER), :] = left[:, t * 128 : (t + 1) * 128]

        for t in range(TILES):
            tile = slice(t * 128, (t + 1) * 128)

            @pl.loop(0, MEMBERS // 8)
            def _(i):
                block = product[t, pl.ds(i * 8 * PER, 8 * PER), :]
                result[q, pl.ds(i * 8, 8), :, tile] = block.reshape(8, PER, 128).astype(bf16)

        for step in X_ORDER:
            there, device = in_plane(step)
            remote(
                result.at[q, pl.ds(there * 16, 16)],
                result_plane.at[q, :, pl.ds(site * PER, PER)],
                out_x_send, out_x_recv.at[q], device,
            )
        pltpu.make_async_copy(
            result.at[q, pl.ds(site * 16, 16)],
            result_plane.at[q, :, pl.ds(site * PER, PER)],
            out_x_recv.at[q],
        ).start()

    def pass_result(q):
        cols = pl.ds(q * WIDE, WIDE)
        pltpu.make_async_copy(result_plane.at[q], result_plane.at[q], out_x_recv.at[q]).wait()
        for step in Z_ORDER:
            there, device = along_z(step)
            remote(
                result_plane.at[q, pl.ds(there * SHARE, SHARE)],
                out_ref.at[:, pl.ds(plane * AREA, AREA), cols],
                out_z_send, out_z_recv, device,
            )
        pltpu.make_async_copy(
            result_plane.at[q, pl.ds(plane * SHARE, SHARE)],
            out_ref.at[:, pl.ds(plane * AREA, AREA), cols],
            out_z_recv,
        ).start()

    for q in range(CHUNKS):
        apply(q)
        if q + 2 * EARLY < CHUNKS:
            pass_state(q + 2 * EARLY)
        if q >= 1:
            pass_result(q - 1)
    pass_result(CHUNKS - 1)

    others = hx_plane.at[pl.ds(0, PLANES - 1)]
    pltpu.make_async_copy(others, others, hx_z_send).wait()
    others = hx_in.at[pl.ds(0, SITES - 1)]
    pltpu.make_async_copy(others, others, hx_x_send).wait()
    others = state_ref.at[:, pl.ds(0, AREA * (PLANES - 1))]
    for sem in (state_z_send, state_x_send, out_x_send, out_z_send):
        pltpu.make_async_copy(others, others, sem).wait()
    pltpu.make_async_copy(out_ref, out_ref, out_z_recv).wait()


def body(hx_ens, obs_value, obs_error, obs_list, obs_count, loc_class, state):
    blocks = LEVEL_OBS // HALF
    dma = pltpu.SemaphoreType.DMA
    any_space = pl.BlockSpec(memory_space=pltpu.HBM)
    return pl.pallas_call(
        kernel,
        out_shape=pltpu.VMEM(state.shape, bf16),
        in_specs=[any_space] * 7,
        out_specs=pl.BlockSpec(memory_space=pltpu.VMEM),
        scratch_shapes=[
            pltpu.VMEM((PLANES, AREA + 2, SHARE, 128), bf16),
            pltpu.VMEM((SITES, PLANES, PER + 2, SHARE, 128), bf16),
            pltpu.VMEM((PER + 2, MEMBERS, 128), bf16),
            pltpu.VMEM((2, 3 * PER, 128), f32),
            pltpu.VMEM((6, 3 * PER, 128), f32),
            pltpu.VMEM((2, PER, CAPACITY), jnp.int32),
            pltpu.VMEM((8, 128), jnp.int32),
            pltpu.VMEM((PER, CAPACITY), f32),
            pltpu.VMEM((PER, GRAM_ROWS, MEMBERS), f32),
            pltpu.VMEM((LEVS - 1, QUART, GRAM_ROWS, MEMBERS), f32),
            pltpu.VMEM((QUART, MEMBERS, MEMBERS), f32),
            pltpu.VMEM((QUART, MEMBERS, MEMBERS), f32),
            pltpu.VMEM((PER, MEMBERS, MEMBERS), bf16),
            pltpu.VMEM((CHUNKS, 16, AREA, WIDE), bf16),
            pltpu.VMEM((CHUNKS, MEMBERS, PER, WIDE), bf16),
            pltpu.VMEM((TILES, MEMBERS * PER, 128), f32),
            pltpu.VMEM((TILES, MEMBERS * PER, 128), f32),
            pltpu.VMEM((CHUNKS, MEMBERS, PER, WIDE), bf16),
            pltpu.VMEM((CHUNKS, 16, AREA, WIDE), bf16),
            dma, dma, dma, dma, dma((9,)),
            dma((3,)), dma((3,)), dma((3,)), dma((3,)),
            dma, dma((CHUNKS,)), dma, dma((CHUNKS,)),
            dma, dma((CHUNKS,)), dma, dma,
        ],
        compiler_params=pltpu.CompilerParams(
            collective_id=0, has_side_effects=True, vmem_limit_bytes=40 << 20
        ),
        cost_estimate=pl.CostEstimate(flops=2_000_000_000, bytes_accessed=20_000_000, transcendentals=0),
    )(
        *(
            pltpu.with_memory_space_constraint(operand, pltpu.HBM)
            for operand in (
                hx_ens.reshape(2, blocks, HALF).transpose(1, 0, 2),
                obs_value.reshape(blocks, HALF),
                obs_error.reshape(blocks, HALF),
                obs_list,
                obs_count.reshape(8, 128),
                loc_class,
                state,
            )
        )
    )


def solution(mesh):
    return jax.shard_map(
        body,
        mesh=mesh,
        in_specs=(
            P("mem", "lev"),
            P("lev"),
            P("lev"),
            P(None, "lev"),
            P(None, "lev"),
            P(None, "lev"),
            P("mem", None, "lev"),
        ),
        out_specs=P("mem", None, "lev"),
        check_vma=False,
    )
```

```python
import functools
import math

import jax
import jax.numpy as jnp
from jax import lax
from jax.experimental import pallas as pl
from jax.experimental.pallas import tpu as pltpu
from jax.sharding import PartitionSpec as P

ITERS = 6
MEMBERS = 128
PLANES = 8
SITES = 8
SHARE = 2
LEVS = 4
PER = 16
AREA = PER * SITES
QUART = PER // LEVS
HALF = 128
CAPACITY = 256
LEVEL_OBS = 131072
COLUMNS = 1024
CHUNKS = 8
WIDE = COLUMNS // CHUNKS
TILES = WIDE // 128
GRAM_ROWS = MEMBERS + 8
Z_ORDER = (1, 7, 2, 6, 3, 5, 4)
X_ORDER = (1, 7, 2, 6, 3, 5, 4)
EARLY = CHUNKS // 4

MESH = pl.DeviceIdType.MESH
HIGHEST = lax.Precision.HIGHEST
f32 = jnp.float32
bf16 = jnp.bfloat16


def dot_nt(a, b, precision=None):
    return lax.dot_general(
        a, b, (((1,), (1,)), ((), ())), precision=precision, preferred_element_type=f32
    )


def dot_nn(a, b, precision=None):
    return jnp.dot(a, b, precision=precision, preferred_element_type=f32)


def kernel(
    hx_ref, value_ref, error_ref, list_ref, count_ref, class_ref, state_ref,
    out_ref,
    hx_plane, hx_in, hx_win, obs_in, pieces, slot_in, count_in, weight,
    gram_out, gram_in, upper, lower, mixers,
    state_plane, state_in, anomaly, product, result, result_plane,
    hx_z_send, hx_z_recv, hx_x_send, hx_x_recv, local_sem,
    gram_send, gram_recv, mix_send, mix_recv,
    state_z_send, state_z_recv, state_x_send, state_x_recv,
    out_x_send, out_x_recv, out_z_send, out_z_recv,
):
    me = lax.axis_index("mem")
    lev = lax.axis_index("lev")
    plane, site = lax.div(me, SITES), lax.rem(me, SITES)
    before, after = lax.rem(me + 63, 64), lax.rem(me + 1, 64)

    def along_z(step):
        there = lax.rem(plane + step, PLANES)
        return there, (there * SITES + site, lev)

    def in_plane(step):
        there = lax.rem(site + step, SITES)
        return there, (plane * SITES + there, lev)

    def greet(device):
        pl.semaphore_signal(barrier, inc=1, device_id=device, device_id_type=MESH)

    barrier = pltpu.get_barrier_semaphore()
    for step in range(1, PLANES):
        greet(along_z(step)[1])
    for step in range(1, SITES):
        greet(in_plane(step)[1])
    for step in range(1, LEVS):
        greet((me, lax.rem(lev + step, LEVS)))

    local = []
    for k, source in enumerate((value_ref, error_ref)):
        for j, block in enumerate((before, me, after)):
            local.append(
                pltpu.make_async_copy(
                    source.at[pl.ds(block * PER, PER)], obs_in.at[k, pl.ds(j * PER, PER)],
                    local_sem.at[k * 3 + j],
                )
            )
    for k, source in enumerate((list_ref, class_ref)):
        local.append(
            pltpu.make_async_copy(source.at[pl.ds(me * PER, PER)], slot_in.at[k], local_sem.at[6 + k])
        )
    local.append(pltpu.make_async_copy(count_ref, count_in, local_sem.at[8]))
    for copy in local:
        copy.start()
    for q in range(CHUNKS):
        pltpu.make_async_copy(
            state_ref.at[:, pl.ds(plane * AREA, AREA), pl.ds(q * WIDE, WIDE)],
            state_plane.at[q, pl.ds(plane * SHARE, SHARE)],
            state_z_recv.at[q],
        ).start()

    def hx_pieces(there):
        blocks = LEVEL_OBS // HALF
        first = there * AREA
        return (
            (hx_ref.at[pl.ds(first, AREA)], hx_plane.at[plane, pl.ds(1, AREA)]),
            (hx_ref.at[pl.ds(lax.rem(first + blocks - 1, blocks), 1)], hx_plane.at[plane, pl.ds(0, 1)]),
            (hx_ref.at[pl.ds(lax.rem(first + AREA, blocks), 1)], hx_plane.at[plane, pl.ds(AREA + 1, 1)]),
        )

    for source, target in hx_pieces(plane):
        pltpu.make_async_copy(source, target, hx_z_recv).start()

    pl.semaphore_wait(barrier, PLANES - 1 + SITES - 1 + LEVS - 1)

    def remote(source, target, send_sem, recv_sem, device):
        pltpu.make_async_remote_copy(
            src_ref=source, dst_ref=target, send_sem=send_sem, recv_sem=recv_sem,
            device_id=device, device_id_type=MESH,
        ).start()

    for step in Z_ORDER:
        there, device = along_z(step)
        for source, target in hx_pieces(there):
            remote(source, target, hx_z_send, hx_z_recv, device)

    def send_state(q):
        for step in Z_ORDER:
            there, device = along_z(step)
            remote(
                state_ref.at[:, pl.ds(there * AREA, AREA), pl.ds(q * WIDE, WIDE)],
                state_plane.at[q, pl.ds(plane * SHARE, SHARE)],
                state_z_send, state_z_recv.at[q], device,
            )

    def pass_state(q):
        pltpu.make_async_copy(state_plane.at[q], state_plane.at[q], state_z_recv.at[q]).wait()
        for step in X_ORDER:
            there, device = in_plane(step)
            remote(
                state_plane.at[q, :, pl.ds(there * PER, PER)],
                state_in.at[q, pl.ds(site * 16, 16)],
                state_x_send, state_x_recv.at[q], device,
            )
        pltpu.make_async_copy(
            state_plane.at[q, :, pl.ds(site * PER, PER)],
            state_in.at[q, pl.ds(site * 16, 16)],
            state_x_recv.at[q],
        ).start()

    for q in range(CHUNKS):
        send_state(q)

    for copy in local:
        copy.wait()
    lanes = lax.broadcasted_iota(jnp.int32, (8, 128), 1)
    rows8 = lax.broadcasted_iota(jnp.int32, (8, 128), 0)
    mine = jnp.sum(jnp.where(rows8 == lax.div(me, 8), count_in[...], 0), axis=0, keepdims=True)
    spots = lax.broadcasted_iota(jnp.int32, (PER, 128), 1) - lax.rem(me, 8) * PER
    patch_rows = lax.broadcasted_iota(jnp.int32, (PER, 128), 0)
    counts = jnp.sum(jnp.where(spots == patch_rows, mine, 0), axis=1, keepdims=True)
    slots = lax.broadcasted_iota(jnp.int32, (PER, CAPACITY), 1)
    scaled = slot_in[1].astype(f32) / 3.0
    weight[...] = jnp.where(slots < counts, jnp.exp(-0.5 * (scaled * scaled)), 0.0)
    del lanes
    for k in range(2):
        rest = obs_in[k]
        for j in range(3):
            piece = rest.astype(bf16).astype(f32)
            pieces[k * 3 + j] = piece
            rest = rest - piece

    pltpu.make_async_copy(hx_plane, hx_plane, hx_z_recv).wait()
    for step in X_ORDER:
        there, device = in_plane(step)
        remote(
            hx_plane.at[:, pl.ds(there * PER, PER + 2)], hx_in.at[site], hx_x_send, hx_x_recv, device
        )
    pltpu.make_async_copy(
        hx_plane.at[:, pl.ds(site * PER, PER + 2)], hx_in.at[site], hx_x_recv
    ).start()
    pltpu.make_async_copy(hx_in, hx_in, hx_x_recv).wait()
    for b in range(PER + 2):
        hx_win[b] = hx_in[:, :, b].astype(f32).reshape(MEMBERS, 128).astype(bf16)

    def patch_gram(p):
        anchor = (me * PER + p - 1) * HALF
        offset = (slot_in[0, pl.ds(p, 1), :] - anchor) & (LEVEL_OBS - 1)
        places = lax.broadcasted_iota(jnp.int32, (HALF, CAPACITY), 0)
        chosen = jnp.zeros((MEMBERS, CAPACITY), f32)
        observed = jnp.zeros((8, CAPACITY), f32)
        for j in range(3):
            table = jnp.where(places + j * HALF == offset, 1.0, 0.0).astype(bf16)
            chosen += dot_nn(hx_win[p + j], table)
            parts = [pieces[k, pl.ds(PER - 1 + p + j, 1), :] for k in range(6)]
            stack = jnp.concatenate(parts + [jnp.zeros((2, HALF), f32)], axis=0)
            observed += dot_nn(stack.astype(bf16), table)
        value = observed[0:1] + observed[1:2] + observed[2:3]
        error = observed[3:4] + observed[4:5] + observed[5:6]
        innov = ((value - chosen) / error * weight[pl.ds(p, 1), :]).astype(bf16).astype(f32)
        average = jnp.mean(innov, axis=0, keepdims=True)
        spread = innov - average
        both = jnp.concatenate([spread, jnp.broadcast_to(average, (8, CAPACITY))], axis=0)
        gram_out[p] = dot_nt(both, spread, HIGHEST)

    @pl.loop(0, PER)
    def _(p):
        patch_gram(p)

    gram_copies = []
    for i in range(1, LEVS):
        target = lax.rem(lev + i, LEVS)
        gram_copies.append(
            pltpu.make_async_remote_copy(
                src_ref=gram_out.at[pl.ds(target * QUART, QUART)],
                dst_ref=gram_in.at[i - 1],
                send_sem=gram_send.at[i - 1], recv_sem=gram_recv.at[i - 1],
                device_id=(me, target), device_id_type=MESH,
            )
        )
    for copy in gram_copies:
        copy.start()
    for q in range(EARLY):
        pass_state(q)
    for copy in gram_copies:
        copy.wait()

    diagonal = lax.broadcasted_iota(jnp.int32, (MEMBERS, MEMBERS), 0) == lax.broadcasted_iota(
        jnp.int32, (MEMBERS, MEMBERS), 1
    )
    identity = jnp.where(diagonal, 1.0, 0.0).astype(f32)
    frobs, pulls = [], []
    for k in range(QUART):
        total = gram_out[lev * QUART + k] + gram_in[0, k] + gram_in[1, k] + gram_in[2, k]
        system = total[:MEMBERS] + (MEMBERS - 1.0) * identity
        squares = jnp.sum(jnp.sum(system * system, axis=0, keepdims=True), axis=1, keepdims=True)
        frob = jnp.sqrt(squares)
        frobs.append(frob)
        pulls.append(-total[MEMBERS : MEMBERS + 1])
        upper[k] = system / frob
        lower[k] = identity

    @pl.loop(0, ITERS)
    def _(step):
        middles = [
            1.5 * identity - 0.5 * dot_nn(lower[k], upper[k], HIGHEST) for k in range(QUART)
        ]
        uppers = [dot_nn(upper[k], middles[k], HIGHEST) for k in range(QUART)]
        lowers = [dot_nn(middles[k], lower[k], HIGHEST) for k in range(QUART)]
        for k in range(QUART):
            upper[k] = uppers[k]
            lower[k] = lowers[k]

    for k in range(QUART):
        root = lower[k] / jnp.sqrt(frobs[k])
        covar = dot_nn(root, root, HIGHEST)
        centre = jnp.sum(covar * pulls[k], axis=1, keepdims=True)
        mixer = math.sqrt(MEMBERS - 1.0) * root + centre - identity
        mixers[lev * QUART + k] = mixer.T.astype(bf16)

    mix_copies = []
    for i in range(1, LEVS):
        target = lax.rem(lev + i, LEVS)
        mix_copies.append(
            pltpu.make_async_remote_copy(
                src_ref=mixers.at[pl.ds(lev * QUART, QUART)],
                dst_ref=mixers.at[pl.ds(lev * QUART, QUART)],
                send_sem=mix_send.at[i - 1], recv_sem=mix_recv.at[i - 1],
                device_id=(me, target), device_id_type=MESH,
            )
        )
    for copy in mix_copies:
        copy.start()
    for q in range(EARLY, 2 * EARLY):
        pass_state(q)
    for copy in mix_copies:
        copy.wait()

    def apply(q):
        pltpu.make_async_copy(state_in.at[q], state_in.at[q], state_x_recv.at[q]).wait()
        for t in range(TILES):
            tile = slice(t * 128, (t + 1) * 128)

            def add(i, total):
                block = state_in[q, pl.ds(i * 8, 8), :, tile].astype(f32)
                return total + jnp.sum(block, axis=0)

            total = lax.fori_loop(0, MEMBERS // 8, add, jnp.zeros((PER, 128), f32))
            mean = total / MEMBERS

            @pl.loop(0, MEMBERS // 8)
            def _(i):
                block = state_in[q, pl.ds(i * 8, 8), :, tile].astype(f32) - mean[None]
                anomaly[t, pl.ds(i * 8 * PER, 8 * PER), :] = block.reshape(8 * PER, 128)

        for p in range(PER):
            right = jnp.concatenate(
                [anomaly[t, pl.ds(p, MEMBERS, stride=PER), :] for t in range(TILES)], axis=1
            ).astype(bf16)
            left = dot_nn(mixers[p], right)
            for t in range(TILES):
                product[t, pl.ds(p, MEMBERS, stride=PER), :] = left[:, t * 128 : (t + 1) * 128]

        for t in range(TILES):
            tile = slice(t * 128, (t + 1) * 128)

            @pl.loop(0, MEMBERS // 8)
            def _(i):
                block = product[t, pl.ds(i * 8 * PER, 8 * PER), :]
                result[q, pl.ds(i * 8, 8), :, tile] = block.reshape(8, PER, 128).astype(bf16)

        for step in X_ORDER:
            there, device = in_plane(step)
            remote(
                result.at[q, pl.ds(there * 16, 16)],
                result_plane.at[q, :, pl.ds(site * PER, PER)],
                out_x_send, out_x_recv.at[q], device,
            )
        pltpu.make_async_copy(
            result.at[q, pl.ds(site * 16, 16)],
            result_plane.at[q, :, pl.ds(site * PER, PER)],
            out_x_recv.at[q],
        ).start()

    def pass_result(q):
        cols = pl.ds(q * WIDE, WIDE)
        pltpu.make_async_copy(result_plane.at[q], result_plane.at[q], out_x_recv.at[q]).wait()
        for step in Z_ORDER:
            there, device = along_z(step)
            remote(
                result_plane.at[q, pl.ds(there * SHARE, SHARE)],
                out_ref.at[:, pl.ds(plane * AREA, AREA), cols],
                out_z_send, out_z_recv, device,
            )
        pltpu.make_async_copy(
            result_plane.at[q, pl.ds(plane * SHARE, SHARE)],
            out_ref.at[:, pl.ds(plane * AREA, AREA), cols],
            out_z_recv,
        ).start()

    for q in range(CHUNKS):
        apply(q)
        if q >= 1:
            pass_result(q - 1)
        if q + 2 * EARLY < CHUNKS:
            pass_state(q + 2 * EARLY)
    pass_result(CHUNKS - 1)

    others = hx_plane.at[pl.ds(0, PLANES - 1)]
    pltpu.make_async_copy(others, others, hx_z_send).wait()
    others = hx_in.at[pl.ds(0, SITES - 1)]
    pltpu.make_async_copy(others, others, hx_x_send).wait()
    others = state_ref.at[:, pl.ds(0, AREA * (PLANES - 1))]
    for sem in (state_z_send, state_x_send, out_x_send, out_z_send):
        pltpu.make_async_copy(others, others, sem).wait()
    pltpu.make_async_copy(out_ref, out_ref, out_z_recv).wait()


def body(hx_ens, obs_value, obs_error, obs_list, obs_count, loc_class, state):
    blocks = LEVEL_OBS // HALF
    dma = pltpu.SemaphoreType.DMA
    any_space = pl.BlockSpec(memory_space=pltpu.HBM)
    return pl.pallas_call(
        kernel,
        out_shape=pltpu.VMEM(state.shape, bf16),
        in_specs=[any_space] * 7,
        out_specs=pl.BlockSpec(memory_space=pltpu.VMEM),
        scratch_shapes=[
            pltpu.VMEM((PLANES, AREA + 2, SHARE, 128), bf16),
            pltpu.VMEM((SITES, PLANES, PER + 2, SHARE, 128), bf16),
            pltpu.VMEM((PER + 2, MEMBERS, 128), bf16),
            pltpu.VMEM((2, 3 * PER, 128), f32),
            pltpu.VMEM((6, 3 * PER, 128), f32),
            pltpu.VMEM((2, PER, CAPACITY), jnp.int32),
            pltpu.VMEM((8, 128), jnp.int32),
            pltpu.VMEM((PER, CAPACITY), f32),
            pltpu.VMEM((PER, GRAM_ROWS, MEMBERS), f32),
            pltpu.VMEM((LEVS - 1, QUART, GRAM_ROWS, MEMBERS), f32),
            pltpu.VMEM((QUART, MEMBERS, MEMBERS), f32),
            pltpu.VMEM((QUART, MEMBERS, MEMBERS), f32),
            pltpu.VMEM((PER, MEMBERS, MEMBERS), bf16),
            pltpu.VMEM((CHUNKS, 16, AREA, WIDE), bf16),
            pltpu.VMEM((CHUNKS, MEMBERS, PER, WIDE), bf16),
            pltpu.VMEM((TILES, MEMBERS * PER, 128), f32),
            pltpu.VMEM((TILES, MEMBERS * PER, 128), f32),
            pltpu.VMEM((CHUNKS, MEMBERS, PER, WIDE), bf16),
            pltpu.VMEM((CHUNKS, 16, AREA, WIDE), bf16),
            dma, dma, dma, dma, dma((9,)),
            dma((3,)), dma((3,)), dma((3,)), dma((3,)),
            dma, dma((CHUNKS,)), dma, dma((CHUNKS,)),
            dma, dma((CHUNKS,)), dma, dma,
        ],
        compiler_params=pltpu.CompilerParams(
            collective_id=0, has_side_effects=True, vmem_limit_bytes=40 << 20
        ),
        cost_estimate=pl.CostEstimate(flops=2_000_000_000, bytes_accessed=20_000_000, transcendentals=0),
    )(
        *(
            pltpu.with_memory_space_constraint(operand, pltpu.HBM)
            for operand in (
                hx_ens.reshape(2, blocks, HALF).transpose(1, 0, 2),
                obs_value.reshape(blocks, HALF),
                obs_error.reshape(blocks, HALF),
                obs_list,
                obs_count.reshape(8, 128),
                loc_class,
                state,
            )
        )
    )


def solution(mesh):
    return jax.shard_map(
        body,
        mesh=mesh,
        in_specs=(
            P("mem", "lev"),
            P("lev"),
            P("lev"),
            P(None, "lev"),
            P(None, "lev"),
            P(None, "lev"),
            P("mem", None, "lev"),
        ),
        out_specs=P("mem", None, "lev"),
        check_vma=False,
    )
```
